32 devices in a mesh: parts: 2 (over y), ctx: 4 (over z), chan: 2 (over x), sub: 2 (over core).
Axes of the slice: x: 2, y: 2, z: 4, core: 2. Of those that a mesh axis runs over, the one named last changes fastest.
Arguments:
- query_rows: bfloat16 [1024, 8192], P(('parts', 'ctx'), ('chan', 'sub')), parts along dimension 0, may hold values from -6 to 6
- key_rows: bfloat16 [1024, 8192], P(('parts', 'ctx'), ('chan', 'sub')), parts along dimension 0, may hold values from -6 to 6
- value_rows: bfloat16 [1024, 8192], P(('parts', 'ctx'), ('chan', 'sub')), parts along dimension 0, may hold values from -6 to 6
- short_filter: float32 [3, 3, 8192], P(None, None, ('chan', 'sub')), may hold values from -3.5 to 3.5
- decay_rate: float32 [16, 8192], P(None, ('chan', 'sub')), may hold values from 9.765625e-05 to 0.05
- residue: float32 [16, 8192], P(None, ('chan', 'sub')), may hold values from -3 to 3
- bypass: float32 [8192], P(('chan', 'sub')), may hold values from -4 to 4
Outputs:
- mixed_out: bfloat16 [1024, 8192], P(('parts', 'ctx'), ('chan', 'sub')), parts along dimension 0
The draws below stay inside these ranges and needn't reach their ends.
There are 2 independent parts, one for each index of `parts`. The reference program is written for one: setup_inputs(seed, part) draws one part's arguments, and reference() takes and returns one part's arrays. A program takes and returns all parts, laid end to end along the dimension named above; an argument that names none is the same for every part. Nothing has to cross between parts.
All inputs are finite; a program needn't handle non-finite values.
Results may differ from the reference program's by a relative error of at most 0.001.
Values may be sent and summed in bfloat16 or wider, within the bound.
A program may use at most 128 MiB of HBM per device.

```python
import math
import jax
import jax.numpy as jnp
from jax import lax

D = 8192
MODES = 16
SHORT = 3
TOKENS = 512


def block_scale(own_key, extent, split, low, high):
    gain, own = 1.0, jax.random.fold_in(own_key, 6)
    for position, parts in split:
        heights = jnp.exp(jax.random.uniform(jax.random.fold_in(own, position), (parts,), jnp.float32, low / len(split), high / len(split)))
        gain = gain * jnp.repeat(heights, extent[position] // parts).reshape([-1 if axis == position else 1 for axis in range(len(extent))])
    return gain


def gaussian(stream_key, dims, scale, bound, pieces=(), held_as=jnp.bfloat16):
    factor_of = block_scale(stream_key, dims, pieces, -0.22, 0.18) if pieces else 1.0
    array = jax.random.normal(stream_key, dims, jnp.float32) * scale * factor_of
    return jnp.minimum(jnp.maximum(array, -bound), bound).astype(held_as)


def setup_inputs(seed: int = 0, part: int = 0) -> dict:
    key_list = jax.random.split(jax.random.key(seed), 8)
    own_keys = jax.random.split(jax.random.fold_in(key_list[7], part), 8)
    return {
        "query_rows": gaussian(own_keys[0], (TOKENS, D), 1.0, 6.0, ((0, 4), (1, 4))),
        "key_rows": gaussian(own_keys[1], (TOKENS, D), 1.0, 6.0, ((0, 4), (1, 4))),
        "value_rows": gaussian(own_keys[2], (TOKENS, D), 1.0, 6.0, ((0, 4), (1, 4))),
        "short_filter": gaussian(key_list[3], (3, SHORT, D), SHORT ** -0.5, 3.5, ((2, 4),), jnp.float32),
        "decay_rate": jnp.clip(jnp.exp(math.log(0.05) - 6.2383246 * jax.random.uniform(key_list[4], (MODES, D), jnp.float32) ** block_scale(key_list[4], (MODES, D), ((1, 4),), -0.2, 0.2)), 9.765625145519152e-05, 0.05),
        "residue": gaussian(key_list[5], (MODES, D), 0.5, 3.0, ((1, 4),), jnp.float32),
        "bypass": gaussian(key_list[6], (D,), 1.0, 4.0, ((0, 4),), jnp.float32),
    }


HIGH = lax.Precision.HIGHEST

def featurize(signal, taps, previous):
    joined = jnp.concatenate([previous, signal], axis=0).astype(jnp.float32)
    length = signal.shape[0]
    return taps[0] * joined[2:] + taps[1] * joined[1:length + 1] + taps[2] * joined[0:length]

def combine(earlier, later):
    return (earlier[0] * later[0], later[0] * earlier[1] + later[1])

def block_tables(decay_rate, residue, block_len):
    offsets = jnp.arange(block_len).astype(jnp.float32)
    mode_gain = jnp.sqrt(-jnp.expm1(-2.0 * decay_rate))
    powers = jnp.exp(-decay_rate[:, None, :] * offsets[None, :, None])
    kernel = jnp.einsum('mlc,mc->lc', powers, residue * mode_gain, precision=HIGH)
    distance = jnp.arange(block_len)[:, None] - jnp.arange(block_len)[None, :]
    toeplitz = jnp.where((distance >= 0)[:, :, None], kernel[jnp.maximum(distance, 0)], jnp.float32(0.0))
    closing = jnp.exp(-decay_rate[:, None, :] * (block_len - 1.0 - offsets)[None, :, None]) * mode_gain[:, None, :]
    opening = residue[:, None, :] * jnp.exp(-decay_rate[:, None, :] * (offsets + 1.0)[None, :, None])
    return (toeplitz, closing, opening)

def block_pass(mixed, decay_rate, residue):
    block_len = 32
    toeplitz, closing, opening = block_tables(decay_rate, residue, block_len)
    blocked = mixed.reshape(-1, block_len, mixed.shape[1])
    inner = jnp.einsum('tsc,bsc->btc', toeplitz, blocked, precision=HIGH)
    block_ends = jnp.einsum('msc,bsc->bmc', closing, blocked, precision=HIGH)
    step_decay = jnp.broadcast_to(jnp.exp(-decay_rate * block_len), block_ends.shape)
    running = lax.associative_scan(combine, (step_decay, block_ends), axis=0)
    entering = jnp.concatenate([jnp.zeros_like(block_ends[:1]), running[1][:-1]], axis=0)
    return (blocked, inner, entering, opening, running[1][-1])

def reference(query_rows, key_rows, value_rows, short_filter, decay_rate, residue, bypass):
    border = jnp.zeros((2, query_rows.shape[1]), jnp.bfloat16)
    query_feat = featurize(query_rows, short_filter[0], border)
    key_feat = featurize(key_rows, short_filter[1], border)
    value_feat = featurize(value_rows, short_filter[2], border)
    gated = key_feat * value_feat
    blocked, inner, entering, opening, device_end = block_pass(gated, decay_rate, residue)
    total = inner + jnp.einsum('mtc,bmc->btc', opening, entering, precision=HIGH) + bypass * blocked
    return (query_feat * total.reshape(gated.shape)).astype(jnp.bfloat16)
```

```python
import functools

import jax
import jax.numpy as jnp
from jax import lax
from jax.experimental import pallas as pl
from jax.experimental.pallas import tpu as pltpu
from jax.sharding import PartitionSpec as P

MESH = pl.DeviceIdType.MESH
SEG = 8
LANES = 128


def kernel(
    n,
    chunks,
    q_ref,
    k_ref,
    v_ref,
    taps_ref,
    decay_ref,
    residue_ref,
    bypass_ref,
    out_ref,
    halo_out,
    halo_in,
    halo,
    stage,
    gated,
    query,
    total,
    local_p,
    arrive_p,
    powers,
    gains,
    seg_decay,
    ends,
    outgoing,
    incoming,
    halo_send,
    halo_recv,
    state_send,
    state_recv,
):
    z = lax.axis_index("ctx")
    tokens, channels = q_ref.shape
    modes = decay_ref.shape[0]
    length = tokens // SEG
    half = channels // 2
    width = channels // chunks
    groups = width // LANES
    has_left = z > 0
    has_right = z < n - 1

    barrier = pltpu.get_barrier_semaphore()

    @pl.when(has_left)
    def _():
        pl.semaphore_signal(barrier, inc=1, device_id={"ctx": z - 1}, device_id_type=MESH)

    @pl.when(has_right)
    def _():
        pl.semaphore_signal(barrier, inc=1, device_id={"ctx": z + 1}, device_id_type=MESH)

    tails = [ref[tokens - 16 :, :].astype(jnp.float32)[14:16] for ref in (q_ref, k_ref, v_ref)]
    rows = jnp.concatenate(tails + [jnp.zeros((2, channels), jnp.float32)], axis=0)
    halo_out[...] = jnp.concatenate([rows[:, :half], rows[:, half:]], axis=0).astype(jnp.bfloat16)

    @pl.when(jnp.logical_and(has_left, has_right))
    def _():
        pl.semaphore_wait(barrier, 2)

    @pl.when(has_left != has_right)
    def _():
        pl.semaphore_wait(barrier, 1)

    def halo_copy():
        return pltpu.make_async_remote_copy(
            src_ref=halo_out,
            dst_ref=halo_in,
            send_sem=halo_send,
            recv_sem=halo_recv,
            device_id={"ctx": z + 1},
            device_id_type=MESH,
        )

    def state_copy(chunk):
        return pltpu.make_async_remote_copy(
            src_ref=outgoing.at[chunk],
            dst_ref=incoming.at[chunk],
            send_sem=state_send.at[chunk],
            recv_sem=state_recv.at[chunk],
            device_id={"ctx": z + 1},
            device_id_type=MESH,
        )

    @pl.when(has_right)
    def _():
        halo_copy().start()

    decay = decay_ref[...]
    powers[...] = jnp.exp(-decay)
    gains[...] = residue_ref[...] * jnp.sqrt(one_minus_exp(2.0 * decay))
    for level in range(3):
        seg_decay[level] = jnp.exp(decay * (-1.0 * length * 2**level))

    @pl.when(jnp.logical_not(has_left))
    def _():
        halo[...] = jnp.zeros_like(halo)
        incoming[...] = jnp.zeros_like(incoming)

    @pl.when(has_left)
    def _():
        halo_copy().wait_recv()
        landed = halo_in[...].astype(jnp.float32)
        halo[:, :half] = landed[:8]
        halo[:, half:] = landed[8:]

    segment = lax.broadcasted_iota(jnp.int32, (SEG, LANES), 0)

    def spread(row):
        return jnp.broadcast_to(row, (SEG, LANES))

    def delayed(value, steps):
        return jnp.where(segment >= steps, pltpu.roll(value, steps, 0), 0.0)

    def featurized(ref, which, slot, lanes):
        stage[slot] = ref[:, lanes].astype(jnp.float32)
        parts = [stage[slot, pl.ds(b, SEG, stride=length), :] for b in range(length)]
        edge = halo[:, lanes]
        first = segment == 0
        before = [
            jnp.where(first, spread(edge[2 * which + r : 2 * which + r + 1]), pltpu.roll(parts[length - 2 + r], 1, 0))
            for r in range(2)
        ]
        joined = before + parts
        taps = [spread(taps_ref[which, i : i + 1, lanes]) for i in range(3)]
        return [taps[0] * joined[b + 2] + taps[1] * joined[b + 1] + taps[2] * joined[b] for b in range(length)]

    def columns(chunk, group):
        return pl.ds(pl.multiple_of(chunk * width + group * LANES, LANES), LANES)

    def inside(group):
        return pl.ds(pl.multiple_of(group * LANES, LANES), LANES)

    def close_chunk(chunk, carry):
        def close_group(group, carry):
            lanes = columns(chunk, group)
            keys = featurized(k_ref, 1, 0, lanes)
            values = featurized(v_ref, 2, 1, lanes)
            signal = [keys[b] * values[b] for b in range(length)]
            for b in range(length):
                gated[b * SEG : (b + 1) * SEG, lanes] = signal[b]
            base = [spread(powers[m : m + 1, lanes]) for m in range(modes)]
            state = [signal[0]] * modes
            for b in range(1, length):
                state = [base[m] * state[m] + signal[b] for m in range(modes)]
            for m in range(modes):
                scan = state[m]
                for level in range(3):
                    scan = scan + spread(seg_decay[level, m : m + 1, lanes]) * delayed(scan, 2**level)
                ends[chunk, m : m + 1, inside(group)] = scan[SEG - 1 :]
                local_p[m * SEG : (m + 1) * SEG, lanes] = spread(gains[m : m + 1, lanes]) * delayed(scan, 1)
            return carry

        lax.fori_loop(0, groups, close_group, 0)

        @pl.when(jnp.logical_and(jnp.logical_not(has_left), has_right))
        def _():
            outgoing[chunk] = ends[chunk]
            state_copy(chunk).start()

        return carry

    lax.fori_loop(0, chunks, close_chunk, 0)

    def relay_chunk(chunk, carry):
        @pl.when(jnp.logical_and(has_left, has_right))
        def _():
            span = pl.ds(pl.multiple_of(chunk * width, LANES), width)
            step = jnp.exp(decay_ref[:, span] * (-1.0 * tokens))
            state_copy(chunk).wait_recv()
            outgoing[chunk] = step * incoming[chunk] + ends[chunk]
            state_copy(chunk).start()

        def local_group(group, carry):
            lanes = columns(chunk, group)
            base = powers[:, lanes]
            term = gains[:, lanes]
            taps = []
            for lag in range(length):
                row = jnp.sum(term, axis=0, keepdims=True)
                if lag == 0:
                    row = row + bypass_ref[:, lanes]
                taps.append(spread(row))
                term = term * base
            signal = [gated[b * SEG : (b + 1) * SEG, lanes] for b in range(length)]
            for b in range(length):
                acc = taps[0] * signal[b]
                for lag in range(1, b + 1):
                    acc = acc + taps[lag] * signal[b - lag]
                total[b * SEG : (b + 1) * SEG, lanes] = acc
            feat = featurized(q_ref, 0, 0, lanes)
            for b in range(length):
                query[b * SEG : (b + 1) * SEG, lanes] = feat[b]
            distance = segment.astype(jnp.float32) * (-1.0 * length)
            for m in range(modes):
                arrive_p[m * SEG : (m + 1) * SEG, lanes] = spread(gains[m : m + 1, lanes]) * jnp.exp(
                    spread(decay_ref[m : m + 1, lanes]) * distance
                )
            return carry

        lax.fori_loop(0, groups, local_group, 0)
        return carry

    lax.fori_loop(0, chunks, relay_chunk, 0)

    def open_chunk(chunk, carry):
        @pl.when(jnp.logical_and(has_left, jnp.logical_not(has_right)))
        def _():
            state_copy(chunk).wait_recv()

        def open_group(group, carry):
            lanes = columns(chunk, group)
            base = [spread(powers[m : m + 1, lanes]) for m in range(modes)]
            term = [
                local_p[m * SEG : (m + 1) * SEG, lanes]
                + arrive_p[m * SEG : (m + 1) * SEG, lanes] * spread(incoming[chunk, m : m + 1, inside(group)])
                for m in range(modes)
            ]
            for b in range(length):
                term = [term[m] * base[m] for m in range(modes)]
                sums = term
                while len(sums) > 1:
                    sums = [x + y for x, y in zip(sums[::2], sums[1::2])] + sums[len(sums) & ~1 :]
                rows = slice(b * SEG, (b + 1) * SEG)
                stage[0, pl.ds(b, SEG, stride=length), :] = query[rows, lanes] * (total[rows, lanes] + sums[0])
            out_ref[:, lanes] = stage[0].astype(jnp.bfloat16)
            return carry

        lax.fori_loop(0, groups, open_group, 0)
        return carry

    lax.fori_loop(0, chunks, open_chunk, 0)

    @pl.when(has_right)
    def _():
        halo_copy().wait_send()

        def drain(chunk, carry):
            state_copy(chunk).wait_send()
            return carry

        lax.fori_loop(0, chunks, drain, 0)


def one_minus_exp(x):
    series = jnp.ones_like(x)
    for order in range(10, 1, -1):
        series = 1.0 - series * x * (1.0 / order)
    return jnp.where(x < 0.5, x * series, 1.0 - jnp.exp(-x))


def local(query_rows, key_rows, value_rows, short_filter, decay_rate, residue, bypass):
    tokens, channels = query_rows.shape
    modes = decay_rate.shape[0]
    chunks = 4
    n = lax.axis_size("ctx")
    length = tokens // SEG
    width = channels // chunks
    f32 = jnp.float32
    return pl.pallas_call(
        functools.partial(kernel, n, chunks),
        out_shape=jax.ShapeDtypeStruct((tokens, channels), jnp.bfloat16),
        in_specs=[pl.BlockSpec(memory_space=pltpu.VMEM)] * 7,
        out_specs=pl.BlockSpec(memory_space=pltpu.VMEM),
        scratch_shapes=[
            pltpu.VMEM((16, channels // 2), jnp.bfloat16),
            pltpu.VMEM((16, channels // 2), jnp.bfloat16),
            pltpu.VMEM((8, channels), f32),
            pltpu.VMEM((2, tokens, LANES), f32),
            pltpu.VMEM((tokens, channels), f32),
            pltpu.VMEM((tokens, channels), f32),
            pltpu.VMEM((tokens, channels), f32),
            pltpu.VMEM((modes * SEG, channels), f32),
            pltpu.VMEM((modes * SEG, channels), f32),
            pltpu.VMEM((modes, channels), f32),
            pltpu.VMEM((modes, channels), f32),
            pltpu.VMEM((3, modes, channels), f32),
            pltpu.VMEM((chunks, modes, width), f32),
            pltpu.VMEM((chunks, modes, width), f32),
            pltpu.VMEM((chunks, modes, width), f32),
            pltpu.SemaphoreType.DMA,
            pltpu.SemaphoreType.DMA,
            pltpu.SemaphoreType.DMA((chunks,)),
            pltpu.SemaphoreType.DMA((chunks,)),
        ],
        compiler_params=pltpu.CompilerParams(
            collective_id=0, has_side_effects=True, vmem_limit_bytes=32 * 1024 * 1024
        ),
        cost_estimate=pl.CostEstimate(
            flops=100 * tokens * channels, bytes_accessed=8 * tokens * channels, transcendentals=0
        ),
    )(query_rows, key_rows, value_rows, short_filter, decay_rate, residue, bypass[None, :])


def solution(mesh):
    placed = (
        P(("parts", "ctx"), ("chan", "sub")),
        P(("parts", "ctx"), ("chan", "sub")),
        P(("parts", "ctx"), ("chan", "sub")),
        P(None, None, ("chan", "sub")),
        P(None, ("chan", "sub")),
        P(None, ("chan", "sub")),
        P(("chan", "sub")),
    )
    return jax.shard_map(
        local,
        mesh=mesh,
        in_specs=placed,
        out_specs=P(("parts", "ctx"), ("chan", "sub")),
        check_vma=False,
    )
```

```python
import functools

import jax
import jax.numpy as jnp
from jax import lax
from jax.experimental import pallas as pl
from jax.experimental.pallas import tpu as pltpu
from jax.sharding import PartitionSpec as P

MESH = pl.DeviceIdType.MESH
SEG = 8
LANES = 128


def kernel(
    n,
    chunks,
    q_hbm,
    k_hbm,
    v_hbm,
    taps_hbm,
    decay_hbm,
    residue_hbm,
    bypass_hbm,
    out_hbm,
    out_ref,
    stores,
    q_ref,
    k_ref,
    v_ref,
    taps_ref,
    decay_ref,
    residue_ref,
    bypass_ref,
    loads,
    firsts,
    fix,
    halo_out,
    halo_in,
    halo,
    stage,
    gated,
    query,
    total,
    local_p,
    arrive_p,
    powers,
    gains,
    seg_decay,
    ends,
    outgoing,
    incoming,
    halo_send,
    halo_recv,
    state_send,
    state_recv,
):
    z = lax.axis_index("ctx")
    tokens, channels = q_hbm.shape
    modes = decay_hbm.shape[0]
    length = tokens // SEG
    half = channels // 2
    width = channels // chunks
    groups = width // LANES
    has_left = z > 0
    has_right = z < n - 1

    tail, body = pl.ds(tokens - 16, 16), pl.ds(0, tokens - 16)
    signals = ((q_hbm, q_ref), (k_hbm, k_ref), (v_hbm, v_ref))
    moves = [(src.at[tail], dst.at[tail]) for src, dst in signals]
    moves += [(decay_hbm, decay_ref), (residue_hbm, residue_ref), (taps_hbm, taps_ref)]
    moves += [(src.at[body], dst.at[body]) for src, dst in signals[1:] + signals[:1]]
    moves += [(bypass_hbm, bypass_ref)]
    copies = [pltpu.make_async_copy(src, dst, loads.at[i]) for i, (src, dst) in enumerate(moves)]
    for copy in copies:
        copy.start()

    barrier = pltpu.get_barrier_semaphore()

    @pl.when(has_left)
    def _():
        pl.semaphore_signal(barrier, inc=1, device_id={"ctx": z - 1}, device_id_type=MESH)

    @pl.when(has_right)
    def _():
        pl.semaphore_signal(barrier, inc=1, device_id={"ctx": z + 1}, device_id_type=MESH)

    for copy in copies[:3]:
        copy.wait()
    tails = [ref[tokens - 16 :, :].astype(jnp.float32)[14:16] for ref in (q_ref, k_ref, v_ref)]
    rows = jnp.concatenate(tails + [jnp.zeros((2, channels), jnp.float32)], axis=0)
    halo_out[...] = jnp.concatenate([rows[:, :half], rows[:, half:]], axis=0).astype(jnp.bfloat16)

    @pl.when(jnp.logical_and(has_left, has_right))
    def _():
        pl.semaphore_wait(barrier, 2)

    @pl.when(has_left != has_right)
    def _():
        pl.semaphore_wait(barrier, 1)

    def halo_copy():
        return pltpu.make_async_remote_copy(
            src_ref=halo_out,
            dst_ref=halo_in,
            send_sem=halo_send,
            recv_sem=halo_recv,
            device_id={"ctx": z + 1},
            device_id_type=MESH,
        )

    def store_copy(chunk):
        span = pl.ds(pl.multiple_of(chunk * width, LANES), width)
        return pltpu.make_async_copy(out_ref.at[:, span], out_hbm.at[:, span], stores.at[chunk])

    def state_copy(chunk):
        return pltpu.make_async_remote_copy(
            src_ref=outgoing.at[chunk],
            dst_ref=incoming.at[chunk],
            send_sem=state_send.at[chunk],
            recv_sem=state_recv.at[chunk],
            device_id={"ctx": z + 1},
            device_id_type=MESH,
        )

    @pl.when(has_right)
    def _():
        halo_copy().start()

    for copy in copies[3:6]:
        copy.wait()
    decay = decay_ref[...]
    powers[...] = jnp.exp(-decay)
    gains[...] = residue_ref[...] * jnp.sqrt(one_minus_exp(2.0 * decay))
    for level in range(3):
        seg_decay[level] = jnp.exp(decay * (-1.0 * length * 2**level))

    for copy in copies[6:8]:
        copy.wait()

    def first_tokens():
        def pair(ref, which):
            rows = ref[0:16, :].astype(jnp.float32)
            now, after = rows[0:1], rows[1:2]
            old, last = halo[2 * which : 2 * which + 1, :], halo[2 * which + 1 : 2 * which + 2, :]
            t0, t1, t2 = [taps_ref[which, i : i + 1, :] for i in range(3)]
            return t0 * now + t1 * last + t2 * old, t0 * after + t1 * now + t2 * last

        keys, values = pair(k_ref, 1), pair(v_ref, 2)
        first, second = keys[0] * values[0], keys[1] * values[1]
        firsts[0:1, :] = first
        firsts[1:2, :] = second
        fix[...] = powers[...] * first + second

    @pl.when(jnp.logical_not(has_left))
    def _():
        halo[...] = jnp.zeros_like(halo)
        incoming[...] = jnp.zeros_like(incoming)
        first_tokens()

    def closing(chunk):
        span = pl.ds(pl.multiple_of(chunk * width, LANES), width)
        return ends[chunk] + jnp.exp(decay_ref[:, span] * (2.0 - tokens)) * fix[:, span]

    segment = lax.broadcasted_iota(jnp.int32, (SEG, LANES), 0)

    def spread(row):
        return jnp.broadcast_to(row, (SEG, LANES))

    def delayed(value, steps):
        return jnp.where(segment >= steps, pltpu.roll(value, steps, 0), 0.0)

    def featurized(ref, which, slot, lanes, with_edge):
        stage[slot] = ref[:, lanes].astype(jnp.float32)
        parts = [stage[slot, pl.ds(b, SEG, stride=length), :] for b in range(length)]
        before = [pltpu.roll(parts[length - 2 + r], 1, 0) for r in range(2)]
        if with_edge:
            edge = [spread(halo[2 * which + r : 2 * which + r + 1, lanes]) for r in range(2)]
            before = [jnp.where(segment == 0, e, x) for e, x in zip(edge, before)]
        joined = before + parts
        taps = [spread(taps_ref[which, i : i + 1, lanes]) for i in range(3)]
        return [taps[0] * joined[b + 2] + taps[1] * joined[b + 1] + taps[2] * joined[b] for b in range(length)]

    def columns(chunk, group):
        return pl.ds(pl.multiple_of(chunk * width + group * LANES, LANES), LANES)

    def inside(group):
        return pl.ds(pl.multiple_of(group * LANES, LANES), LANES)

    def close_chunk(chunk, carry):
        def close_group(group, carry):
            lanes = columns(chunk, group)
            keys = featurized(k_ref, 1, 0, lanes, False)
            values = featurized(v_ref, 2, 1, lanes, False)
            signal = [keys[b] * values[b] for b in range(length)]
            signal[:2] = [jnp.where(segment == 0, 0.0, value) for value in signal[:2]]
            for b in range(length):
                gated[b * SEG : (b + 1) * SEG, lanes] = signal[b]
            base = [spread(powers[m : m + 1, lanes]) for m in range(modes)]
            state = [signal[0]] * modes
            for b in range(1, length):
                state = [base[m] * state[m] + signal[b] for m in range(modes)]
            for m in range(modes):
                scan = state[m]
                for level in range(3):
                    scan = scan + spread(seg_decay[level, m : m + 1, lanes]) * delayed(scan, 2**level)
                ends[chunk, m : m + 1, inside(group)] = scan[SEG - 1 :]
                local_p[m * SEG : (m + 1) * SEG, lanes] = scan
            return carry

        lax.fori_loop(0, groups, close_group, 0)

        @pl.when(jnp.logical_and(jnp.logical_not(has_left), has_right))
        def _():
            outgoing[chunk] = closing(chunk)
            state_copy(chunk).start()

        return carry

    lax.fori_loop(0, chunks, close_chunk, 0)

    @pl.when(has_left)
    def _():
        halo_copy().wait_recv()
        landed = halo_in[...].astype(jnp.float32)
        halo[:, :half] = landed[:8]
        halo[:, half:] = landed[8:]
        first_tokens()

    for copy in copies[8:]:
        copy.wait()

    def relay_chunk(chunk, carry):
        @pl.when(jnp.logical_and(has_left, has_right))
        def _():
            span = pl.ds(pl.multiple_of(chunk * width, LANES), width)
            step = jnp.exp(decay_ref[:, span] * (-1.0 * tokens))
            state_copy(chunk).wait_recv()
            outgoing[chunk] = step * incoming[chunk] + closing(chunk)
            state_copy(chunk).start()

        def local_group(group, carry):
            lanes = columns(chunk, group)
            base = powers[:, lanes]
            term = gains[:, lanes]
            taps = []
            for lag in range(length):
                row = jnp.sum(term, axis=0, keepdims=True)
                if lag == 0:
                    row = row + bypass_ref[:, lanes]
                taps.append(spread(row))
                term = term * base
            signal = [gated[b * SEG : (b + 1) * SEG, lanes] for b in range(length)]
            signal[:2] = [jnp.where(segment == 0, spread(firsts[b : b + 1, lanes]), signal[b]) for b in range(2)]
            for b in range(length):
                acc = taps[0] * signal[b]
                for lag in range(1, b + 1):
                    acc = acc + taps[lag] * signal[b - lag]
                total[b * SEG : (b + 1) * SEG, lanes] = acc
            feat = featurized(q_ref, 0, 0, lanes, True)
            for b in range(length):
                query[b * SEG : (b + 1) * SEG, lanes] = feat[b]
            distance = segment.astype(jnp.float32) * (-1.0 * length)
            lift = jnp.exp(2.0 * decay_ref[:, lanes]) * fix[:, lanes]
            for m in range(modes):
                rows = slice(m * SEG, (m + 1) * SEG)
                gain = spread(gains[m : m + 1, lanes])
                arrive = gain * jnp.exp(spread(decay_ref[m : m + 1, lanes]) * distance)
                arrive_p[rows, lanes] = arrive
                earlier = pltpu.roll(local_p[rows, lanes], 1, 0)
                local_p[rows, lanes] = jnp.where(
                    segment >= 1, gain * earlier + arrive * spread(lift[m : m + 1]), 0.0
                )
            return carry

        lax.fori_loop(0, groups, local_group, 0)
        return carry

    lax.fori_loop(0, chunks, relay_chunk, 0)

    def open_chunk(chunk, carry):
        @pl.when(jnp.logical_and(has_left, jnp.logical_not(has_right)))
        def _():
            state_copy(chunk).wait_recv()

        def open_group(group, carry):
            lanes = columns(chunk, group)
            base = [spread(powers[m : m + 1, lanes]) for m in range(modes)]
            term = [
                local_p[m * SEG : (m + 1) * SEG, lanes]
                + arrive_p[m * SEG : (m + 1) * SEG, lanes] * spread(incoming[chunk, m : m + 1, inside(group)])
                for m in range(modes)
            ]
            for b in range(length):
                term = [term[m] * base[m] for m in range(modes)]
                sums = term
                while len(sums) > 1:
                    sums = [x + y for x, y in zip(sums[::2], sums[1::2])] + sums[len(sums) & ~1 :]
                rows = slice(b * SEG, (b + 1) * SEG)
                stage[0, pl.ds(b, SEG, stride=length), :] = query[rows, lanes] * (total[rows, lanes] + sums[0])
            out_ref[:, lanes] = stage[0].astype(jnp.bfloat16)
            return carry

        lax.fori_loop(0, groups, open_group, 0)
        store_copy(chunk).start()
        return carry

    lax.fori_loop(0, chunks, open_chunk, 0)

    @pl.when(has_right)
    def _():
        halo_copy().wait_send()

        def drain(chunk, carry):
            state_copy(chunk).wait_send()
            return carry

        lax.fori_loop(0, chunks, drain, 0)

    def finish(chunk, carry):
        store_copy(chunk).wait()
        return carry

    lax.fori_loop(0, chunks, finish, 0)


def one_minus_exp(x):
    series = jnp.ones_like(x)
    for order in range(10, 1, -1):
        series = 1.0 - series * x * (1.0 / order)
    return jnp.where(x < 0.5, x * series, 1.0 - jnp.exp(-x))


def local(query_rows, key_rows, value_rows, short_filter, decay_rate, residue, bypass):
    tokens, channels = query_rows.shape
    modes = decay_rate.shape[0]
    chunks = next(c for c in (8, 4, 2, 1) if channels % (c * LANES) == 0)
    n = lax.axis_size("ctx")
    length = tokens // SEG
    width = channels // chunks
    f32 = jnp.float32
    return pl.pallas_call(
        functools.partial(kernel, n, chunks),
        out_shape=jax.ShapeDtypeStruct((tokens, channels), jnp.bfloat16),
        in_specs=[pl.BlockSpec(memory_space=pltpu.HBM)] * 7,
        out_specs=pl.BlockSpec(memory_space=pltpu.HBM),
        scratch_shapes=[
            pltpu.VMEM((tokens, channels), jnp.bfloat16),
            pltpu.SemaphoreType.DMA((chunks,)),
            pltpu.VMEM((tokens, channels), jnp.bfloat16),
            pltpu.VMEM((tokens, channels), jnp.bfloat16),
            pltpu.VMEM((tokens, channels), jnp.bfloat16),
            pltpu.VMEM(short_filter.shape, f32),
            pltpu.VMEM((modes, channels), f32),
            pltpu.VMEM((modes, channels), f32),
            pltpu.VMEM((1, channels), f32),
            pltpu.SemaphoreType.DMA((10,)),
            pltpu.VMEM((8, channels), f32),
            pltpu.VMEM((modes, channels), f32),
            pltpu.VMEM((16, channels // 2), jnp.bfloat16),
            pltpu.VMEM((16, channels // 2), jnp.bfloat16),
            pltpu.VMEM((8, channels), f32),
            pltpu.VMEM((2, tokens, LANES), f32),
            pltpu.VMEM((tokens, channels), f32),
            pltpu.VMEM((tokens, channels), f32),
            pltpu.VMEM((tokens, channels), f32),
            pltpu.VMEM((modes * SEG, channels), f32),
            pltpu.VMEM((modes * SEG, channels), f32),
            pltpu.VMEM((modes, channels), f32),
            pltpu.VMEM((modes, channels), f32),
            pltpu.VMEM((3, modes, channels), f32),
            pltpu.VMEM((chunks, modes, width), f32),
            pltpu.VMEM((chunks, modes, width), f32),
            pltpu.VMEM((chunks, modes, width), f32),
            pltpu.SemaphoreType.DMA,
            pltpu.SemaphoreType.DMA,
            pltpu.SemaphoreType.DMA((chunks,)),
            pltpu.SemaphoreType.DMA((chunks,)),
        ],
        compiler_params=pltpu.CompilerParams(
            collective_id=0, has_side_effects=True, vmem_limit_bytes=60 * 1024 * 1024
        ),
        cost_estimate=pl.CostEstimate(
            flops=100 * tokens * channels, bytes_accessed=8 * tokens * channels, transcendentals=0
        ),
    )(query_rows, key_rows, value_rows, short_filter, decay_rate, residue, bypass[None, :])


def solution(mesh):
    placed = (
        P(("parts", "ctx"), ("chan", "sub")),
        P(("parts", "ctx"), ("chan", "sub")),
        P(("parts", "ctx"), ("chan", "sub")),
        P(None, None, ("chan", "sub")),
        P(None, ("chan", "sub")),
        P(None, ("chan", "sub")),
        P(("chan", "sub")),
    )
    return jax.shard_map(
        local,
        mesh=mesh,
        in_specs=placed,
        out_specs=P(("parts", "ctx"), ("chan", "sub")),
        check_vma=False,
    )
```

```python
import functools

import jax
import jax.numpy as jnp
from jax import lax
from jax.experimental import pallas as pl
from jax.experimental.pallas import tpu as pltpu
from jax.sharding import PartitionSpec as P

MESH = pl.DeviceIdType.MESH
SEG = 8
LANES = 128


def kernel(
    n,
    chunks,
    q_hbm,
    k_hbm,
    v_hbm,
    taps_hbm,
    decay_hbm,
    residue_hbm,
    bypass_hbm,
    out_hbm,
    out_ref,
    stores,
    q_ref,
    k_ref,
    v_ref,
    taps_ref,
    decay_ref,
    residue_ref,
    bypass_ref,
    loads,
    firsts,
    fix,
    halo_out,
    halo_in,
    halo,
    stage,
    gated,
    query,
    total,
    local_p,
    arrive_p,
    powers,
    gains,
    seg_decay,
    ends,
    outgoing,
    incoming,
    halo_send,
    halo_recv,
    state_send,
    state_recv,
):
    z = lax.axis_index("ctx")
    tokens, channels = q_hbm.shape
    modes = decay_hbm.shape[0]
    length = tokens // SEG
    half = channels // 2
    width = channels // chunks
    groups = width // LANES
    has_left = z > 0
    has_right = z < n - 1

    tail, body = pl.ds(tokens - 16, 16), pl.ds(0, tokens - 16)
    signals = ((q_hbm, q_ref), (k_hbm, k_ref), (v_hbm, v_ref))
    moves = [(src.at[tail], dst.at[tail]) for src, dst in signals]
    moves += [(decay_hbm, decay_ref), (residue_hbm, residue_ref), (taps_hbm, taps_ref)]
    moves += [(src.at[body], dst.at[body]) for src, dst in signals[1:] + signals[:1]]
    moves += [(bypass_hbm, bypass_ref)]
    copies = [pltpu.make_async_copy(src, dst, loads.at[i]) for i, (src, dst) in enumerate(moves)]
    for copy in copies:
        copy.start()

    barrier = pltpu.get_barrier_semaphore()

    @pl.when(has_left)
    def _():
        pl.semaphore_signal(barrier, inc=1, device_id={"ctx": z - 1}, device_id_type=MESH)

    @pl.when(has_right)
    def _():
        pl.semaphore_signal(barrier, inc=1, device_id={"ctx": z + 1}, device_id_type=MESH)

    for copy in copies[:3]:
        copy.wait()
    tails = [ref[tokens - 16 :, :].astype(jnp.float32)[14:16] for ref in (q_ref, k_ref, v_ref)]
    rows = jnp.concatenate(tails + [jnp.zeros((2, channels), jnp.float32)], axis=0)
    halo_out[...] = jnp.concatenate([rows[:, :half], rows[:, half:]], axis=0).astype(jnp.bfloat16)

    @pl.when(jnp.logical_and(has_left, has_right))
    def _():
        pl.semaphore_wait(barrier, 2)

    @pl.when(has_left != has_right)
    def _():
        pl.semaphore_wait(barrier, 1)

    def halo_copy():
        return pltpu.make_async_remote_copy(
            src_ref=halo_out,
            dst_ref=halo_in,
            send_sem=halo_send,
            recv_sem=halo_recv,
            device_id={"ctx": z + 1},
            device_id_type=MESH,
        )

    def store_copy(chunk):
        span = pl.ds(pl.multiple_of(chunk * width, LANES), width)
        return pltpu.make_async_copy(out_ref.at[:, span], out_hbm.at[:, span], stores.at[chunk])

    def state_copy(chunk):
        return pltpu.make_async_remote_copy(
            src_ref=outgoing.at[chunk],
            dst_ref=incoming.at[chunk],
            send_sem=state_send.at[chunk],
            recv_sem=state_recv.at[chunk],
            device_id={"ctx": z + 1},
            device_id_type=MESH,
        )

    @pl.when(has_right)
    def _():
        halo_copy().start()

    for copy in copies[3:6]:
        copy.wait()
    decay = decay_ref[...]
    powers[...] = jnp.exp(-decay)
    gains[...] = residue_ref[...] * jnp.sqrt(one_minus_exp(2.0 * decay))
    for level in range(3):
        seg_decay[level] = jnp.exp(decay * (-1.0 * length * 2**level))

    for copy in copies[6:8]:
        copy.wait()

    def first_tokens():
        def pair(ref, which):
            rows = ref[0:16, :].astype(jnp.float32)
            now, after = rows[0:1], rows[1:2]
            old, last = halo[2 * which : 2 * which + 1, :], halo[2 * which + 1 : 2 * which + 2, :]
            t0, t1, t2 = [taps_ref[which, i : i + 1, :] for i in range(3)]
            return t0 * now + t1 * last + t2 * old, t0 * after + t1 * now + t2 * last

        keys, values = pair(k_ref, 1), pair(v_ref, 2)
        first, second = keys[0] * values[0], keys[1] * values[1]
        firsts[0:1, :] = first
        firsts[1:2, :] = second
        fix[...] = powers[...] * first + second

    @pl.when(jnp.logical_not(has_left))
    def _():
        halo[...] = jnp.zeros_like(halo)
        incoming[...] = jnp.zeros_like(incoming)
        first_tokens()

    def closing(chunk):
        span = pl.ds(pl.multiple_of(chunk * width, LANES), width)
        return ends[chunk] + jnp.exp(decay_ref[:, span] * (2.0 - tokens)) * fix[:, span]

    segment = lax.broadcasted_iota(jnp.int32, (SEG, LANES), 0)

    def spread(row):
        return jnp.broadcast_to(row, (SEG, LANES))

    def delayed(value, steps):
        return jnp.where(segment >= steps, pltpu.roll(value, steps, 0), 0.0)

    def featurized(ref, which, slot, lanes, with_edge):
        stage[slot] = ref[:, lanes].astype(jnp.float32)
        parts = [stage[slot, pl.ds(b, SEG, stride=length), :] for b in range(length)]
        before = [pltpu.roll(parts[length - 2 + r], 1, 0) for r in range(2)]
        if with_edge:
            edge = [spread(halo[2 * which + r : 2 * which + r + 1, lanes]) for r in range(2)]
            before = [jnp.where(segment == 0, e, x) for e, x in zip(edge, before)]
        joined = before + parts
        taps = [spread(taps_ref[which, i : i + 1, lanes]) for i in range(3)]
        return [taps[0] * joined[b + 2] + taps[1] * joined[b + 1] + taps[2] * joined[b] for b in range(length)]

    def columns(chunk, group):
        return pl.ds(pl.multiple_of(chunk * width + group * LANES, LANES), LANES)

    def inside(group):
        return pl.ds(pl.multiple_of(group * LANES, LANES), LANES)

    def close_chunk(chunk, carry):
        def close_group(group, carry):
            lanes = columns(chunk, group)
            keys = featurized(k_ref, 1, 0, lanes, False)
            values = featurized(v_ref, 2, 1, lanes, False)
            signal = [keys[b] * values[b] for b in range(length)]
            signal[:2] = [jnp.where(segment == 0, 0.0, value) for value in signal[:2]]
            for b in range(length):
                gated[b * SEG : (b + 1) * SEG, lanes] = signal[b]
            base = [spread(powers[m : m + 1, lanes]) for m in range(modes)]
            state = [signal[0]] * modes
            for b in range(1, length):
                state = [base[m] * state[m] + signal[b] for m in range(modes)]
            for m in range(modes):
                scan = state[m]
                for level in range(3):
                    scan = scan + spread(seg_decay[level, m : m + 1, lanes]) * delayed(scan, 2**level)
                ends[chunk, m : m + 1, inside(group)] = scan[SEG - 1 :]
                local_p[m * SEG : (m + 1) * SEG, lanes] = scan
            return carry

        lax.fori_loop(0, groups, close_group, 0)

        @pl.when(jnp.logical_and(jnp.logical_not(has_left), has_right))
        def _():
            outgoing[chunk] = closing(chunk)
            state_copy(chunk).start()

        return carry

    lax.fori_loop(0, chunks, close_chunk, 0)

    @pl.when(has_left)
    def _():
        halo_copy().wait_recv()
        landed = halo_in[...].astype(jnp.float32)
        halo[:, :half] = landed[:8]
        halo[:, half:] = landed[8:]
        first_tokens()

    for copy in copies[8:]:
        copy.wait()

    def relay_chunk(chunk, carry):
        @pl.when(jnp.logical_and(has_left, has_right))
        def _():
            span = pl.ds(pl.multiple_of(chunk * width, LANES), width)
            step = jnp.exp(decay_ref[:, span] * (-1.0 * tokens))
            state_copy(chunk).wait_recv()
            outgoing[chunk] = step * incoming[chunk] + closing(chunk)
            state_copy(chunk).start()

        def local_group(group, carry):
            lanes = columns(chunk, group)
            base = powers[:, lanes]
            term = gains[:, lanes]
            taps = []
            for lag in range(length):
                row = jnp.sum(term, axis=0, keepdims=True)
                if lag == 0:
                    row = row + bypass_ref[:, lanes]
                taps.append(spread(row))
                term = term * base
            signal = [gated[b * SEG : (b + 1) * SEG, lanes] for b in range(length)]
            signal[:2] = [jnp.where(segment == 0, spread(firsts[b : b + 1, lanes]), signal[b]) for b in range(2)]
            for b in range(length):
                acc = taps[0] * signal[b]
                for lag in range(1, b + 1):
                    acc = acc + taps[lag] * signal[b - lag]
                total[b * SEG : (b + 1) * SEG, lanes] = acc
            feat = featurized(q_ref, 0, 0, lanes, True)
            for b in range(length):
                query[b * SEG : (b + 1) * SEG, lanes] = feat[b]
            distance = segment.astype(jnp.float32) * (-1.0 * length)
            lift = jnp.exp(2.0 * decay_ref[:, lanes]) * fix[:, lanes]
            for m in range(modes):
                rows = slice(m * SEG, (m + 1) * SEG)
                gain = spread(gains[m : m + 1, lanes])
                arrive = gain * jnp.exp(spread(decay_ref[m : m + 1, lanes]) * distance)
                arrive_p[rows, lanes] = arrive
                earlier = pltpu.roll(local_p[rows, lanes], 1, 0)
                local_p[rows, lanes] = jnp.where(
                    segment >= 1, gain * earlier + arrive * spread(lift[m : m + 1]), 0.0
                )
            return carry

        lax.fori_loop(0, groups, local_group, 0)
        return carry

    lax.fori_loop(0, chunks, relay_chunk, 0)

    def open_chunk(chunk, carry):
        @pl.when(jnp.logical_and(has_left, jnp.logical_not(has_right)))
        def _():
            state_copy(chunk).wait_recv()

        def open_group(group, carry):
            lanes = columns(chunk, group)
            base = [spread(powers[m : m + 1, lanes]) for m in range(modes)]
            term = [
                local_p[m * SEG : (m + 1) * SEG, lanes]
                + arrive_p[m * SEG : (m + 1) * SEG, lanes] * spread(incoming[chunk, m : m + 1, inside(group)])
                for m in range(modes)
            ]
            for b in range(length):
                term = [term[m] * base[m] for m in range(modes)]
                sums = term
                while len(sums) > 1:
                    sums = [x + y for x, y in zip(sums[::2], sums[1::2])] + sums[len(sums) & ~1 :]
                rows = slice(b * SEG, (b + 1) * SEG)
                stage[0, pl.ds(b, SEG, stride=length), :] = query[rows, lanes] * (total[rows, lanes] + sums[0])
            out_ref[:, lanes] = stage[0].astype(jnp.bfloat16)
            return carry

        lax.fori_loop(0, groups, open_group, 0)
        store_copy(chunk).start()
        return carry

    lax.fori_loop(0, chunks, open_chunk, 0)

    @pl.when(has_right)
    def _():
        halo_copy().wait_send()

        def drain(chunk, carry):
            state_copy(chunk).wait_send()
            return carry

        lax.fori_loop(0, chunks, drain, 0)

    def finish(chunk, carry):
        store_copy(chunk).wait()
        return carry

    lax.fori_loop(0, chunks, finish, 0)


def one_minus_exp(x):
    series = jnp.ones_like(x)
    for order in range(10, 1, -1):
        series = 1.0 - series * x * (1.0 / order)
    return jnp.where(x < 0.5, x * series, 1.0 - jnp.exp(-x))


def local(query_rows, key_rows, value_rows, short_filter, decay_rate, residue, bypass):
    tokens, channels = query_rows.shape
    modes = decay_rate.shape[0]
    chunks = next(c for c in (16, 8, 4, 2, 1) if channels % (c * LANES) == 0)
    n = lax.axis_size("ctx")
    length = tokens // SEG
    width = channels // chunks
    f32 = jnp.float32
    return pl.pallas_call(
        functools.partial(kernel, n, chunks),
        out_shape=jax.ShapeDtypeStruct((tokens, channels), jnp.bfloat16),
        in_specs=[pl.BlockSpec(memory_space=pltpu.HBM)] * 7,
        out_specs=pl.BlockSpec(memory_space=pltpu.HBM),
        scratch_shapes=[
            pltpu.VMEM((tokens, channels), jnp.bfloat16),
            pltpu.SemaphoreType.DMA((chunks,)),
            pltpu.VMEM((tokens, channels), jnp.bfloat16),
            pltpu.VMEM((tokens, channels), jnp.bfloat16),
            pltpu.VMEM((tokens, channels), jnp.bfloat16),
            pltpu.VMEM(short_filter.shape, f32),
            pltpu.VMEM((modes, channels), f32),
            pltpu.VMEM((modes, channels), f32),
            pltpu.VMEM((1, channels), f32),
            pltpu.SemaphoreType.DMA((10,)),
            pltpu.VMEM((8, channels), f32),
            pltpu.VMEM((modes, channels), f32),
            pltpu.VMEM((16, channels // 2), jnp.bfloat16),
            pltpu.VMEM((16, channels // 2), jnp.bfloat16),
            pltpu.VMEM((8, channels), f32),
            pltpu.VMEM((2, tokens, LANES), f32),
            pltpu.VMEM((tokens, channels), f32),
            pltpu.VMEM((tokens, channels), f32),
            pltpu.VMEM((tokens, channels), f32),
            pltpu.VMEM((modes * SEG, channels), f32),
            pltpu.VMEM((modes * SEG, channels), f32),
            pltpu.VMEM((modes, channels), f32),
            pltpu.VMEM((modes, channels), f32),
            pltpu.VMEM((3, modes, channels), f32),
            pltpu.VMEM((chunks, modes, width), f32),
            pltpu.VMEM((chunks, modes, width), f32),
            pltpu.VMEM((chunks, modes, width), f32),
            pltpu.SemaphoreType.DMA,
            pltpu.SemaphoreType.DMA,
            pltpu.SemaphoreType.DMA((chunks,)),
            pltpu.SemaphoreType.DMA((chunks,)),
        ],
        compiler_params=pltpu.CompilerParams(
            collective_id=0, has_side_effects=True, vmem_limit_bytes=60 * 1024 * 1024
        ),
        cost_estimate=pl.CostEstimate(
            flops=100 * tokens * channels, bytes_accessed=8 * tokens * channels, transcendentals=0
        ),
    )(query_rows, key_rows, value_rows, short_filter, decay_rate, residue, bypass[None, :])


def solution(mesh):
    placed = (
        P(("parts", "ctx"), ("chan", "sub")),
        P(("parts", "ctx"), ("chan", "sub")),
        P(("parts", "ctx"), ("chan", "sub")),
        P(None, None, ("chan", "sub")),
        P(None, ("chan", "sub")),
        P(None, ("chan", "sub")),
        P(("chan", "sub")),
    )
    return jax.shard_map(
        local,
        mesh=mesh,
        in_specs=placed,
        out_specs=P(("parts", "ctx"), ("chan", "sub")),
        check_vma=False,
    )
```
